256 devices in a mesh: dom: 8 (over y, x_hi), ref: 32 (over x_lo, z, core).
Axes of the slice: x: 4 (x_hi: 2, x_lo: 2; x = x_hi * 2 + x_lo), y: 4, z: 8, core: 2. Of those that a mesh axis runs over, the one named last changes fastest.
Arguments:
- particles: bfloat16 [2048, 16384], P(('dom', 'ref')), may hold values from -6 to 6
- offsets: int32 [2048, 2], P(('dom', 'ref')), may hold values from -6 to 6
- groups: int32 [2048], P(('dom', 'ref')), may hold values from 0 to 31
- precision: float32 [2048], P(('dom', 'ref')), may hold values from 0.05 to 16
- references: bfloat16 [8192, 16384], P('ref'), may hold values from -0.1796875 to 0.1796875
- ctf: float32 [32, 16384], replicated, may hold values from 0.25 to 1.75
- regularizer: float32 [8192], P('ref'), may hold values from 0.05 to 0.5
Outputs:
- new_references: float32 [16384, 8192], P('dom', 'ref')
- log_evidence: float32 [2048], P(('dom', 'ref'))
The draws below stay inside these ranges and needn't reach their ends.
All inputs are finite; a program needn't handle non-finite values.
Results may differ from the reference program's by a relative error of at most 0.023.
Values may be sent and summed in bfloat16 or wider, within the bound.
No kernel may reach another device: no remote copies, remote signals or barrier semaphores. Data moves between devices by JAX's collectives and lax.ppermute only.
A program may use at most 128 MiB of HBM per device.

```python
import math
import jax
import jax.numpy as jnp
from jax import lax

IMG = 128
PIX = 16384
REFS = 8192
PARTICLES = 2048
GROUPS = 32
SHIFT = 6
N_DOM = 8


def draw_precision(key, part):
    key = jax.random.fold_in(key, 7)
    first = jax.random.fold_in(key, 0)
    values = jnp.exp(jax.random.uniform(first, (PARTICLES,), jnp.float32, jnp.log(0.05), jnp.log(0.3)))
    position = jnp.arange(PARTICLES, dtype=jnp.int32) // (PARTICLES // N_DOM)
    fraction = position.astype(jnp.float32) / max(N_DOM - 1, 1)
    values = values * (1.0 + 2.0 * fraction)
    return values


def set_ends(entries, stream_key, low, top_value):
    extent = entries.shape
    index_at = [jax.random.randint(jax.random.fold_in(stream_key, axis), (), 0, extent[axis]) for axis in range(len(extent))]
    entries = entries.at[tuple(index_at)].set(low)
    longest = extent.index(max(extent))
    index_at[longest] = (index_at[longest] + 1) % extent[longest]
    return entries.at[tuple(index_at)].set(top_value)


def block_levels(rng, extent, pieces, least, high):
    def one(axis_at, blocks):
        draws = jax.random.uniform(jax.random.fold_in(jax.random.fold_in(rng, 6), axis_at), (blocks,), jnp.float32, least / len(pieces), high / len(pieces))
        return jnp.repeat(jnp.exp(draws), extent[axis_at] // blocks).reshape((-1,) + (1,) * (len(extent) - axis_at - 1))

    level = one(*pieces[0])
    for cut in pieces[1:]:
        level = level * one(*cut)
    return level


def normal_values(own_key, dims, deviation, limit, shards=(), kind=jnp.bfloat16):
    values = jax.random.normal(own_key, dims, jnp.float32) * deviation
    if len(shards) > 0:
        values = block_levels(own_key, dims, shards, -0.22, 0.18) * values
    return jnp.clip(values, min=-limit, max=limit).astype(kind)


def setup_inputs(seed: int = 0) -> dict:
    streams_of = jax.random.split(jax.random.key(seed), 8)
    particles = normal_values(streams_of[0], (PARTICLES, PIX), 1.0, 6.0, ((0, 256),))
    offsets = set_ends(jax.random.randint(streams_of[1], (PARTICLES, 2), 0 - SHIFT, SHIFT + 1), jax.random.fold_in(streams_of[1], 1), 0 - SHIFT, SHIFT).astype(jnp.int32)
    groups = set_ends(jax.random.randint(streams_of[2], (PARTICLES,), 0, GROUPS), jax.random.fold_in(streams_of[2], 1), 0, GROUPS - 1).astype(jnp.int32)
    precision = draw_precision(jax.random.fold_in(streams_of[7], 71), 0)
    references = normal_values(streams_of[4], (REFS, PIX), 0.03, 0.1796875, ((0, 32),))
    ctf = jnp.clip(1.0 + 0.15 * jax.random.normal(streams_of[5], (GROUPS, PIX), jnp.float32), 0.25, 1.75)
    regularizer = jnp.clip(jnp.exp(math.log(0.5) - 2.3025851 * jax.random.uniform(streams_of[6], (REFS,), jnp.float32) ** block_levels(streams_of[6], (REFS,), ((0, 32),), -0.2, 0.2)), 0.05, 0.5)
    return {"particles": particles, "offsets": offsets, "groups": groups, "precision": precision, "references": references, "ctf": ctf, "regularizer": regularizer}


def shift_images(images, offsets, side):
    squares = images.reshape(images.shape[0], side, side)

    def single(image, offset):
        return jnp.roll(image, (offset[0], offset[1]), axis=(0, 1))

    return jax.vmap(single)(squares, offsets).reshape(images.shape[0], side * side)


def reference(particles, offsets, groups, precision, references, ctf, regularizer):
    shifted = shift_images(particles, offsets, IMG)
    filtered = (ctf[groups] * shifted.astype(jnp.float32)).astype(jnp.bfloat16)
    ref_float = references.astype(jnp.float32)
    ctf_square = ctf * ctf
    quad = jnp.dot(ctf_square, (ref_float * ref_float).T, precision=lax.Precision.HIGHEST)
    inner = jnp.dot(filtered, references.T, preferred_element_type=jnp.float32)
    scores = precision[:, None] * (inner - 0.5 * quad[groups])
    log_evidence = jax.nn.logsumexp(scores, axis=1)
    weights = jnp.exp(scores - log_evidence[:, None])
    rounded = weights.astype(jnp.bfloat16)
    numerator = jnp.dot(filtered.T, rounded, preferred_element_type=jnp.float32)
    onehot = (groups[:, None] == jnp.arange(GROUPS, dtype=jnp.int32)[None, :]).astype(jnp.float32)
    group_weights = jnp.dot(onehot.T, weights, precision=lax.Precision.HIGHEST)
    denominator = jnp.dot(ctf_square.T, group_weights, precision=lax.Precision.HIGHEST)
    new_references = numerator / (denominator + regularizer[None, :])
    return new_references, log_evidence
```

```python
import functools

import jax
import jax.numpy as jnp
import numpy as np
from jax import lax
from jax.experimental import pallas as pl
from jax.experimental.pallas import tpu as pltpu
from jax.sharding import PartitionSpec as P

IMG = 128
EXTRA = 128


def split3(value):
    high = lax.reduce_precision(value, 8, 7)
    rest = value - high
    mid = lax.reduce_precision(rest, 8, 7)
    low = rest - mid
    return high, mid, low


def filter_kernel(offsets, groups, parts, particles, ctf, out, planes, rows):
    images = particles.shape[0]
    side = IMG
    shares, _, width = out.shape
    pixels = width - EXTRA
    per_share = pixels // side
    for line in range(side):
        planes[pl.ds(line, images, stride=side), :] = particles[
            :, line * side : (line + 1) * side
        ].astype(jnp.float32)
    for n in range(images):
        image = planes[n * side : (n + 1) * side, :]
        down = lax.rem(offsets[n, 0] + side, side)
        right = lax.rem(offsets[n, 1] + side, side)
        image = pltpu.roll(image, down, 0)
        image = pltpu.roll(image, right, 1)
        planes[n * side : (n + 1) * side, :] = image
        rows[n : n + 1, :] = ctf[pl.ds(groups[n], 1), :]
    lane = lax.broadcasted_iota(jnp.int32, (1, EXTRA), 1)
    slot = lax.broadcasted_iota(jnp.int32, (images, EXTRA), 0)
    extra = jnp.zeros((images, EXTRA), jnp.float32)
    for n in range(images):
        hot = jnp.where((lane < 96) & (lax.rem(lane, 32) == groups[n]), 1.0, 0.0)
        for part in range(3):
            hot = jnp.where(lane == 96 + part, parts[part, n], hot)
        extra = jnp.where(slot == n, hot, extra)
    extra = extra.astype(jnp.bfloat16)
    for share in range(shares):
        for line in range(per_share):
            at = share * per_share + line
            value = planes[pl.ds(at, images, stride=side), :] * rows[:, at * side : (at + 1) * side]
            out[share, :, line * side : (line + 1) * side] = value.astype(jnp.bfloat16)
        out[share, :, pixels:] = extra


def filtered_shares(particles, offsets, groups, precision, ctf, shares):
    images, pixels = particles.shape
    parts = jnp.stack(split3(precision))
    smem = pl.BlockSpec(memory_space=pltpu.SMEM)
    vmem = pl.BlockSpec(memory_space=pltpu.VMEM)
    return pl.pallas_call(
        filter_kernel,
        out_shape=jax.ShapeDtypeStruct((shares, images, pixels // shares + EXTRA), jnp.bfloat16),
        in_specs=[smem, smem, smem, vmem, vmem],
        out_specs=vmem,
        scratch_shapes=[
            pltpu.VMEM((images * IMG, IMG), jnp.float32),
            pltpu.VMEM((images, pixels), jnp.float32),
        ],
        compiler_params=pltpu.CompilerParams(vmem_limit_bytes=24 << 20),
    )(offsets, groups, parts, particles, ctf)


def ring_tables(mesh):
    n_ref, n_dom = mesh.shape["ref"], mesh.shape["dom"]
    depth = n_ref // 4

    def along(step):
        return [(i, (i // (2 * depth)) * 2 * depth + (i + 2 * step) % (2 * depth)) for i in range(n_ref)]

    high = n_dom // 2
    return {
        "core": ("ref", [(i, i ^ 1) for i in range(n_ref)]),
        "side": ("ref", [(i, (i + 2 * depth) % n_ref) for i in range(n_ref)]),
        "up": ("ref", along(1)),
        "down": ("ref", along(-1)),
        "far": ("dom", [(i, i ^ 1) for i in range(n_dom)]),
        "y1": ("dom", [(i, (i + 2) % n_dom) for i in range(n_dom)]),
        "y2": ("dom", [(i, (i + 4) % n_dom) for i in range(n_dom)]),
        "y3": ("dom", [(i, (i + 6) % n_dom) for i in range(n_dom)]),
    }


def turned(value, by, axis):
    size = value.shape[axis]
    return lax.dynamic_slice_in_dim(jnp.concatenate([value, value], axis), by, size, axis)


def local(tables, particles, offsets, groups, precision, references, ctf, regularizer):
    def send(name, value):
        axis, pairs = tables[name]
        return lax.ppermute(value, axis, pairs)

    dom = lax.axis_index("dom")
    ref = lax.axis_index("ref")
    n_dom = lax.axis_size("dom")
    n_ref = lax.axis_size("ref")
    depth = n_ref // 4
    x_at, z_at, c_at = ref // (2 * depth), (ref // 2) % depth, ref % 2
    y_at, far_at = dom // 2, dom % 2
    n_y = n_dom // 2
    own, pixels = particles.shape
    share = pixels // n_dom
    n_group = ctf.shape[0]
    n_own_ref = references.shape[0]
    first = dom * share

    pieces = filtered_shares(particles, offsets, groups, precision, ctf, n_dom)

    ref_share = lax.dynamic_slice_in_dim(references, first, share, 1)
    ctf_share = lax.dynamic_slice_in_dim(ctf, first, share, 1)
    ctf_square = ctf_share * ctf_share
    ref_float = ref_share.astype(jnp.float32)
    quad = lax.dot_general(
        ref_float * ref_float, ctf_square, (((1,), (1,)), ((), ())), precision=lax.Precision.HIGHEST
    )
    penalty = jnp.concatenate(split3(-0.5 * quad), axis=1)
    penalty = jnp.pad(penalty, ((0, 0), (0, EXTRA - 3 * n_group))).astype(jnp.bfloat16)
    table = jnp.concatenate([ref_share, penalty], axis=1)
    table_x = send("side", table)
    tables4 = jnp.concatenate([table, send("core", table), table_x, send("core", table_x)], axis=0)

    block = lax.all_to_all(pieces, "dom", 0, 0, tiled=True)
    block = block.reshape(n_dom * own, share + EXTRA)
    half = block.shape[0] // 2

    held = {0: [block[:half], block[half:]]}
    up, down = held[0], held[0]
    for step in range(1, depth // 2 + 1):
        up = [send("up", v) for v in up]
        held[depth - step] = up
        if step < depth // 2:
            down = [send("down", v) for v in down]
            held[step] = down

    near = [o for o in range(depth) if min(o, depth - o) < 3]
    late = [o for o in range(depth) if min(o, depth - o) >= 3]

    def scores_of(places):
        rows = jnp.concatenate([v for o in places for v in held[o]], axis=0)
        inner = lax.dot_general(
            rows, tables4, (((1,), (1,)), ((), ())), preferred_element_type=jnp.float32
        )
        noise = rows[:, share + 96 : share + 99].astype(jnp.float32)
        noise = noise[:, 0] + noise[:, 1] + noise[:, 2]
        part = (inner * noise[:, None]).reshape(len(places), n_y, 2, own, 4 * n_own_ref)

        def of(y):
            return lax.dynamic_index_in_dim(part, y % n_y, 1, keepdims=False)

        total = of(y_at)
        for k in range(1, n_y):
            total = total + send(f"y{k}", of(y_at + k))
        kept = lax.dynamic_index_in_dim(total, far_at, 1, keepdims=False)
        given = lax.dynamic_index_in_dim(total, 1 - far_at, 1, keepdims=False)
        score = kept + send("far", given)
        top = jnp.max(score, axis=2)
        powers = jnp.exp(score - top[:, :, None])
        return rows, top, jnp.sum(powers, axis=2), powers.astype(jnp.bfloat16)

    def dom_gather(value):
        pair = jnp.stack([value, send("far", value)])
        return jnp.stack([pair] + [send(f"y{n_y - k}", pair) for k in range(1, n_y)])

    def spread(powers):
        places = powers.shape[0]
        powers = powers.reshape(places, own, 4, n_own_ref)
        given = send("side", powers[:, :, 2:])
        both = jnp.stack([powers[:, :, :2], given])
        other = send("core", both[:, :, :, 1])
        return dom_gather(jnp.stack([both[:, :, :, 0], other], axis=1))

    rows1, top1, sum1, pow1 = scores_of(near)
    rows2, top2, sum2, pow2 = scores_of(late)
    spread1 = spread(pow1)
    spread2 = spread(pow2)

    def by_place(one, two):
        found = {**{o: one[..., i, :] for i, o in enumerate(near)}, **{o: two[..., i, :] for i, o in enumerate(late)}}
        return jnp.stack([found[o] for o in range(depth)], axis=-2)

    stats = jnp.stack([by_place(top1, top2), by_place(sum1, sum2)])
    stats = turned(stats, (depth - z_at) % depth, 1).reshape(1, 2 * depth * own)
    stats = lax.all_to_all(jnp.broadcast_to(stats, (n_ref, stats.shape[1])), "ref", 0, 0, tiled=True)
    stats = stats.reshape(2, depth, 2, 2, depth, own)
    tops, sums = stats[:, :, :, 0], stats[:, :, :, 1]
    highest = jnp.max(tops, axis=1)
    total = jnp.sum(sums * jnp.exp(tops - highest[:, None]), axis=1)
    evidence = highest + jnp.log(total)
    mine = lax.dynamic_index_in_dim(tops, z_at, 1, keepdims=False)
    both = jnp.stack([jnp.exp(mine - evidence), evidence])
    both = turned(turned(turned(both, x_at, 1), c_at, 2), z_at, 3)
    log_evidence = both[1, 0, 0, 0]
    scale = dom_gather(both[0])

    powers = {}
    for places, part in ((near, spread1), (late, spread2)):
        for i, o in enumerate(places):
            powers[o] = part[:, :, :, :, i]
    powers = jnp.stack([powers[o] for o in range(depth)], axis=4)
    weights = (powers.astype(jnp.float32) * scale[..., None]).astype(jnp.bfloat16)
    weights = turned(turned(weights, (n_y - y_at) % n_y, 0), far_at, 1)

    def all_columns(rows):
        two = jnp.stack([rows, send("side", rows)])
        return jnp.stack([two, send("core", two)], axis=1)

    lines = []
    hots = []
    for places, rows in ((near, rows1), (late, rows2)):
        lines.append(all_columns(rows).reshape(-1, rows.shape[1]))
        part = jnp.stack([weights[:, :, :, :, o] for o in places], axis=4)
        part = part.transpose(2, 3, 4, 0, 1, 5, 6)
        hots.append(part.reshape(-1, n_own_ref))
    lines = jnp.concatenate(lines, axis=0)
    hots = jnp.concatenate(hots, axis=0)
    sums = lax.dot_general(
        lines, hots, (((0,), (0,)), ((), ())), preferred_element_type=jnp.float32
    )
    numerator = sums[:share]
    group_weights = sums[share : share + n_group]
    denominator = lax.dot_general(
        ctf_square, group_weights, (((0,), (0,)), ((), ())), precision=lax.Precision.HIGHEST
    )
    new_references = numerator / (denominator + regularizer[None, :])
    return new_references, log_evidence


def solution(mesh):
    return jax.shard_map(
        functools.partial(local, ring_tables(mesh)),
        mesh=mesh,
        in_specs=(
            P(("dom", "ref"), None),
            P(("dom", "ref"), None),
            P(("dom", "ref")),
            P(("dom", "ref")),
            P("ref", None),
            P(),
            P("ref"),
        ),
        out_specs=(P("dom", "ref"), P(("dom", "ref"))),
        check_vma=False,
    )
```

```python
import functools

import jax
import jax.numpy as jnp
import numpy as np
from jax import lax
from jax.experimental import pallas as pl
from jax.experimental.pallas import tpu as pltpu
from jax.sharding import PartitionSpec as P

IMG = 128
EXTRA = 128


VMEM = pl.BlockSpec(memory_space=pltpu.VMEM)
SMEM = pl.BlockSpec(memory_space=pltpu.SMEM)
ANY = pl.BlockSpec(memory_space=pl.ANY)
ROOM = pltpu.CompilerParams(vmem_limit_bytes=24 << 20)
WIDE = pltpu.CompilerParams(vmem_limit_bytes=56 << 20)


def rounded(value):
    return value.astype(jnp.bfloat16).astype(jnp.float32)


def split3(value):
    high = rounded(value)
    rest = value - high
    mid = rounded(rest)
    return high, mid, rest - mid


def filter_kernel(offsets, groups, precision, particles, ctf, out, planes, images, rows, sems):
    count, side = images.shape[0], IMG
    shares, _, width = out.shape
    pixels = width - EXTRA
    per_share = pixels // side
    whole = pltpu.make_async_copy(particles, images, sems.at[count])
    whole.start()
    copies = []
    for n in range(count):
        copy = pltpu.make_async_copy(ctf.at[pl.ds(groups[n], 1)], rows.at[pl.ds(n, 1)], sems.at[n])
        copy.start()
        copies.append(copy)
    lane = lax.broadcasted_iota(jnp.int32, (1, EXTRA), 1)
    slot = lax.broadcasted_iota(jnp.int32, (count, EXTRA), 0)
    extra = jnp.zeros((count, EXTRA), jnp.float32)
    for n in range(count):
        hot = jnp.where((lane < 96) & (lax.rem(lane, 32) == groups[n]), 1.0, 0.0)
        for part, value in enumerate(split3(jnp.full((1, EXTRA), precision[n], jnp.float32))):
            hot = jnp.where(lane == 96 + part, value, hot)
        extra = jnp.where(slot == n, hot, extra)
    extra = extra.astype(jnp.bfloat16)
    whole.wait()
    for line in range(side):
        planes[pl.ds(line, count, stride=side), :] = images[
            :, line * side : (line + 1) * side
        ].astype(jnp.float32)
    for n in range(count):
        image = planes[n * side : (n + 1) * side, :]
        image = pltpu.roll(image, lax.rem(offsets[0, n] + side, side), 0)
        image = pltpu.roll(image, lax.rem(offsets[1, n] + side, side), 1)
        planes[n * side : (n + 1) * side, :] = image
    for copy in copies:
        copy.wait()
    for share in range(shares):
        for line in range(per_share):
            at = share * per_share + line
            value = planes[pl.ds(at, count, stride=side), :] * rows[:, at * side : (at + 1) * side]
            out[share, :, line * side : (line + 1) * side] = value.astype(jnp.bfloat16)
        out[share, :, pixels:] = extra


def filtered_shares(particles, offsets, groups, precision, ctf, shares):
    images, pixels = particles.shape
    return pl.pallas_call(
        filter_kernel,
        out_shape=jax.ShapeDtypeStruct((shares, images, pixels // shares + EXTRA), jnp.bfloat16),
        in_specs=[SMEM, SMEM, SMEM, ANY, ANY],
        out_specs=VMEM,
        scratch_shapes=[
            pltpu.VMEM((images * IMG, IMG), jnp.float32),
            pltpu.VMEM((images, pixels), jnp.bfloat16),
            pltpu.VMEM((images, pixels), jnp.float32),
            pltpu.SemaphoreType.DMA((images + 1,)),
        ],
        compiler_params=WIDE,
    )(offsets.T, groups, precision, particles, ctf)


def table_kernel(place, references, ctf, table, part, filters, sems):
    share = part.shape[1]
    group = ctf.shape[0]
    first = pl.multiple_of(place[2] * share, share)
    one = pltpu.make_async_copy(ctf.at[:, pl.ds(first, share)], filters, sems.at[0])
    two = pltpu.make_async_copy(references.at[:, pl.ds(first, share)], part, sems.at[1])
    one.start()
    two.start()
    one.wait()
    two.wait()
    step = 256
    total = jnp.zeros((part.shape[0], EXTRA), jnp.float32)
    for at in range(0, share, step):
        value = part[:, at : at + step]
        table[:, at : at + step] = value
        value = value.astype(jnp.float32)
        value = value * value
        high = rounded(value)
        square = filters[:, at : at + step]
        square = jnp.concatenate(
            list(split3(square * square)) + [jnp.zeros((EXTRA - 3 * group, step), jnp.float32)], axis=0
        ).astype(jnp.bfloat16)
        for some in (high, value - high):
            total = total + lax.dot_general(
                some.astype(jnp.bfloat16), square, (((1,), (1,)), ((), ())), preferred_element_type=jnp.float32
            )
    quad = total + pltpu.roll(total, EXTRA - group, 1) + pltpu.roll(total, EXTRA - 2 * group, 1)
    lane = lax.broadcasted_iota(jnp.int32, quad.shape, 1)
    high, mid, low = split3(jnp.where(lane < group, -0.5 * quad, 0.0))
    table[:, share:] = (high + pltpu.roll(mid, group, 1) + pltpu.roll(low, 2 * group, 1)).astype(jnp.bfloat16)


def share_table(place, references, ctf, shares):
    rows, share = references.shape[0], references.shape[1] // shares
    return pl.pallas_call(
        table_kernel,
        out_shape=jax.ShapeDtypeStruct((rows, share + EXTRA), jnp.bfloat16),
        in_specs=[SMEM, ANY, ANY],
        out_specs=VMEM,
        scratch_shapes=[
            pltpu.VMEM((rows, share), jnp.bfloat16),
            pltpu.VMEM((ctf.shape[0], share), jnp.float32),
            pltpu.SemaphoreType.DMA((2,)),
        ],
        compiler_params=WIDE,
        cost_estimate=pl.CostEstimate(flops=1 << 29, bytes_accessed=8 << 20, transcendentals=0),
    )(place, references, ctf)


def score_kernel(counts, *refs):
    count = sum(counts)
    blocks, tables = refs[:count], refs[count : count + 4]
    out, lines = refs[count + 4 :]
    n_dom, rows, width = out.shape[0], out.shape[1], out.shape[2] // 4
    own = rows // len(counts)
    at = 0
    for block in blocks:
        lines[at : at + block.shape[0], :] = block[...]
        at += block.shape[0]
    share = lines.shape[1] - EXTRA
    extra = lines[:, share:].astype(jnp.float32)
    noise = extra[:, 96:97] + extra[:, 97:98] + extra[:, 98:99]
    for q, table in enumerate(tables):
        part = lax.dot_general(
            lines[...], table[...], (((1,), (1,)), ((), ())), preferred_element_type=jnp.float32
        )
        part = part * noise
        for o in range(len(counts)):
            for d in range(n_dom):
                at = (o * n_dom + d) * own
                out[d, o * own : (o + 1) * own, q * width : (q + 1) * width] = part[at : at + own, :]


def places_of(z_at, rows, own):
    line = lax.broadcasted_iota(jnp.int32, (rows, 2 * rows), 0)
    lane = lax.broadcasted_iota(jnp.int32, (rows, 2 * rows), 1)
    return lane, lax.rem(line + z_at * own, rows)


def soften_kernel(place, parts, score, stats):
    value = parts[0]
    for d in range(1, parts.shape[0]):
        value = value + parts[d]
    score[...] = value
    rows = value.shape[0]
    top = jnp.max(value, axis=1, keepdims=True)
    total = jnp.sum(jnp.exp(value - top), axis=1, keepdims=True)
    lane, target = places_of(place[1], rows, rows // stats.shape[0])
    both = jnp.where(lane == target, top, 0.0) + jnp.where(lane == target + rows, total, 0.0)
    stats[...] = jnp.broadcast_to(jnp.sum(both, axis=0, keepdims=True)[None], stats.shape)


def weigh_kernel(place, score, stats, spread, evidence, table):
    x_c, z_at = place[0], place[1]
    rows = score.shape[0]
    own = rows // stats.shape[0]
    tops = stats[...]
    sums = pltpu.roll(tops, rows, 1)
    highest = jnp.max(tops, axis=0, keepdims=True)
    total = jnp.sum(sums * jnp.exp(tops - highest), axis=0, keepdims=True)
    logged = highest + jnp.log(total)
    evidence[...] = logged
    lane, target = places_of(z_at, rows, own)
    column = jnp.sum(jnp.where(lane == target, logged, 0.0), axis=1, keepdims=True)
    value = jnp.exp(score[...] - column)
    for o in range(rows // own):
        at = pl.multiple_of(lax.rem(z_at + o, rows // own) * own, own)
        table[pl.ds(at, own), :] = value[o * own : (o + 1) * own, :]
    width = table.shape[1] // 4
    for q in range(4):
        part = table[:, q * width : (q + 1) * width].astype(jnp.bfloat16)
        for d in range(spread.shape[0] // 4):
            spread[d * 4 + (q ^ x_c)] = part


def divide_kernel(sums, square, regularizer, out):
    share, width = out.shape
    n_group = square.shape[1] // 4
    high = sums[share : share + n_group, :]
    first = high.astype(jnp.bfloat16).astype(jnp.float32)
    second = (high - first).astype(jnp.bfloat16)
    first = first.astype(jnp.bfloat16)
    factors = jnp.concatenate([first, first, second, jnp.zeros_like(second)], axis=0)
    step = 256
    for at in range(0, share, step):
        bottom = jnp.dot(square[at : at + step, :], factors, preferred_element_type=jnp.float32)
        out[at : at + step, :] = sums[at : at + step, :] / (bottom + regularizer[...])


def ring_tables(mesh):
    n_ref, n_dom = mesh.shape["ref"], mesh.shape["dom"]
    depth = n_ref // 4

    def along(step):
        return [(i, (i // (2 * depth)) * 2 * depth + (i + 2 * step) % (2 * depth)) for i in range(n_ref)]

    return {
        "core": ("ref", [(i, i ^ 1) for i in range(n_ref)]),
        "side": ("ref", [(i, (i + 2 * depth) % n_ref) for i in range(n_ref)]),
        "up": ("ref", along(1)),
        "down": ("ref", along(-1)),
        "column": [
            [x * 2 * depth + z * 2 + c for z in range(depth)] for x in range(2) for c in range(2)
        ],
        "same_z": [
            [d * n_ref + x * 2 * depth + z * 2 + c for d in range(n_dom) for x in range(2) for c in range(2)]
            for z in range(depth)
        ],
    }


def local(tables, particles, offsets, groups, precision, references, ctf, regularizer):
    def send(name, value):
        axis, pairs = tables[name]
        return lax.ppermute(value, axis, pairs)

    dom = lax.axis_index("dom")
    ref = lax.axis_index("ref")
    n_dom = lax.axis_size("dom")
    n_ref = lax.axis_size("ref")
    depth = n_ref // 4
    x_at, z_at, c_at = ref // (2 * depth), (ref // 2) % depth, ref % 2
    own, pixels = particles.shape
    share = pixels // n_dom
    n_group = ctf.shape[0]
    n_own_ref = references.shape[0]

    pieces = filtered_shares(particles, offsets, groups, precision, ctf, n_dom)

    place = jnp.stack([x_at * 2 + c_at, z_at, dom])
    table = share_table(lax.optimization_barrier((place, pieces))[0], references, ctf, n_dom)
    ctf_share = lax.dynamic_slice_in_dim(ctf, dom * share, share, 1)
    square_t = (ctf_share * ctf_share).T
    square_high = lax.reduce_precision(square_t, 8, 7)
    square = jnp.concatenate(
        [square_high, square_t - square_high, square_high, jnp.zeros_like(square_t)], axis=1
    ).astype(jnp.bfloat16)
    block = lax.all_to_all(pieces, "dom", 0, 0, tiled=True)
    block = block.reshape(n_dom * own, share + EXTRA)
    half = block.shape[0] // 2
    table_x = send("side", table)
    beside = send("side", block)

    held = {0: [block]}
    up = down = block
    for step in range(1, depth // 2):
        up, down = send("up", up), send("down", down)
        held[depth - step] = [up]
        held[step] = [down]
    table_x = lax.optimization_barrier((table_x, up, down))[0]
    beside = lax.optimization_barrier((beside, up, down))[0]
    held[depth // 2] = [send("up", up[:half]), send("down", down[half:])]
    beside = lax.all_gather(beside, "ref", axis=0, tiled=True, axis_index_groups=tables["column"])
    tables4 = [table, send("core", table), table_x, send("core", table_x)]

    rows = depth * own
    blocks = [held[o] for o in range(depth)]
    counts = [len(v) for v in blocks]
    parts, mine = pl.pallas_call(
        functools.partial(score_kernel, counts),
        out_shape=(
            jax.ShapeDtypeStruct((n_dom, rows, 4 * n_own_ref), jnp.float32),
            jax.ShapeDtypeStruct((n_dom * rows, share + EXTRA), jnp.bfloat16),
        ),
        in_specs=[VMEM] * (sum(counts) + 4),
        out_specs=(VMEM, VMEM),
        compiler_params=ROOM,
    )(*[v for some in blocks for v in some], *tables4)
    parts = lax.all_to_all(parts, "dom", 0, 0, tiled=True)

    score, stats = pl.pallas_call(
        soften_kernel,
        out_shape=(
            jax.ShapeDtypeStruct((rows, 4 * n_own_ref), jnp.float32),
            jax.ShapeDtypeStruct((depth, 1, 2 * rows), jnp.float32),
        ),
        in_specs=[SMEM, VMEM],
        out_specs=(VMEM, VMEM),
        compiler_params=ROOM,
    )(place, parts)
    stats = lax.all_to_all(stats, "ref", 0, 0, tiled=True, axis_index_groups=tables["column"])
    weights, evidence = pl.pallas_call(
        weigh_kernel,
        out_shape=(
            jax.ShapeDtypeStruct((4 * n_dom, rows, n_own_ref), jnp.bfloat16),
            jax.ShapeDtypeStruct((1, 2 * rows), jnp.float32),
        ),
        in_specs=[SMEM, VMEM, VMEM],
        out_specs=(VMEM, VMEM),
        scratch_shapes=[pltpu.VMEM((rows, 4 * n_own_ref), jnp.float32)],
        compiler_params=ROOM,
    )(place, score, stats.reshape(depth, 2 * rows))
    log_evidence = lax.dynamic_slice(evidence, (0, z_at * own), (1, own)).reshape(own)
    weights = lax.all_to_all(
        weights, ("dom", "ref"), 0, 0, tiled=True, axis_index_groups=tables["same_z"]
    )
    weights = weights.reshape(n_dom, 2, 2, depth, own, n_own_ref)

    def order(x, c, turn):
        some = lax.dynamic_slice(
            weights, (0, x, c, 0, 0, 0), (n_dom, 1, 1, depth, own, n_own_ref)
        ).reshape(n_dom, depth, own, n_own_ref)
        if turn:
            some = lax.dynamic_slice_in_dim(jnp.concatenate([some, some], axis=1), z_at, depth, 1)
        return some.transpose(1, 0, 2, 3).reshape(-1, n_own_ref)

    sums = 0.0
    for some, side in ((mine, 0), (beside, 1)):
        for rows_of, core in ((some, 0), (send("core", some), 1)):
            weight = order((x_at + side) % 2, (c_at + core) % 2, side == 0)
            sums = sums + lax.dot_general(
                rows_of, weight, (((0,), (0,)), ((), ())), preferred_element_type=jnp.float32
            )
    new_references = pl.pallas_call(
        divide_kernel,
        out_shape=jax.ShapeDtypeStruct((share, n_own_ref), jnp.float32),
        in_specs=[VMEM, VMEM, VMEM],
        out_specs=VMEM,
        compiler_params=ROOM,
    )(sums, square, regularizer[None, :])
    return new_references, log_evidence


def solution(mesh):
    return jax.shard_map(
        functools.partial(local, ring_tables(mesh)),
        mesh=mesh,
        in_specs=(
            P(("dom", "ref"), None),
            P(("dom", "ref"), None),
            P(("dom", "ref")),
            P(("dom", "ref")),
            P("ref", None),
            P(),
            P("ref"),
        ),
        out_specs=(P("dom", "ref"), P(("dom", "ref"))),
        check_vma=False,
    )
```

```python
import functools

import jax
import jax.numpy as jnp
import numpy as np
from jax import lax
from jax.experimental import pallas as pl
from jax.experimental.pallas import tpu as pltpu
from jax.sharding import PartitionSpec as P

IMG = 128
EXTRA = 128


VMEM = pl.BlockSpec(memory_space=pltpu.VMEM)
SMEM = pl.BlockSpec(memory_space=pltpu.SMEM)
ANY = pl.BlockSpec(memory_space=pl.ANY)
ROOM = pltpu.CompilerParams(vmem_limit_bytes=24 << 20)
WIDE = pltpu.CompilerParams(vmem_limit_bytes=56 << 20)


def rounded(value):
    return value.astype(jnp.bfloat16).astype(jnp.float32)


def split3(value):
    high = rounded(value)
    rest = value - high
    mid = rounded(rest)
    return high, mid, rest - mid


def filter_kernel(offsets, groups, precision, particles, ctf, out, planes, images, rows, sems):
    count, side = images.shape[0], IMG
    shares, _, width = out.shape
    pixels = width - EXTRA
    per_share = pixels // side
    whole = pltpu.make_async_copy(particles, images, sems.at[count])
    whole.start()
    copies = []
    for n in range(count):
        copy = pltpu.make_async_copy(ctf.at[pl.ds(groups[n], 1)], rows.at[pl.ds(n, 1)], sems.at[n])
        copy.start()
        copies.append(copy)
    lane = lax.broadcasted_iota(jnp.int32, (1, EXTRA), 1)
    slot = lax.broadcasted_iota(jnp.int32, (count, EXTRA), 0)
    extra = jnp.zeros((count, EXTRA), jnp.float32)
    for n in range(count):
        hot = jnp.where((lane < 96) & (lax.rem(lane, 32) == groups[n]), 1.0, 0.0)
        for part, value in enumerate(split3(jnp.full((1, EXTRA), precision[n], jnp.float32))):
            hot = jnp.where(lane == 96 + part, value, hot)
        extra = jnp.where(slot == n, hot, extra)
    extra = extra.astype(jnp.bfloat16)
    whole.wait()
    for line in range(side):
        planes[pl.ds(line, count, stride=side), :] = images[
            :, line * side : (line + 1) * side
        ].astype(jnp.float32)
    for n in range(count):
        image = planes[n * side : (n + 1) * side, :]
        image = pltpu.roll(image, lax.rem(offsets[0, n] + side, side), 0)
        image = pltpu.roll(image, lax.rem(offsets[1, n] + side, side), 1)
        planes[n * side : (n + 1) * side, :] = image
    for copy in copies:
        copy.wait()
    for share in range(shares):
        for line in range(per_share):
            at = share * per_share + line
            value = planes[pl.ds(at, count, stride=side), :] * rows[:, at * side : (at + 1) * side]
            out[share, :, line * side : (line + 1) * side] = value.astype(jnp.bfloat16)
        out[share, :, pixels:] = extra


def filtered_shares(particles, offsets, groups, precision, ctf, shares):
    images, pixels = particles.shape
    return pl.pallas_call(
        filter_kernel,
        out_shape=jax.ShapeDtypeStruct((shares, images, pixels // shares + EXTRA), jnp.bfloat16),
        in_specs=[SMEM, SMEM, SMEM, ANY, ANY],
        out_specs=VMEM,
        scratch_shapes=[
            pltpu.VMEM((images * IMG, IMG), jnp.float32),
            pltpu.VMEM((images, pixels), jnp.bfloat16),
            pltpu.VMEM((images, pixels), jnp.float32),
            pltpu.SemaphoreType.DMA((images + 1,)),
        ],
        compiler_params=WIDE,
    )(offsets.T, groups, precision, particles, ctf)


def table_kernel(place, references, ctf, table, part, filters, sems):
    share = part.shape[1]
    group = ctf.shape[0]
    first = pl.multiple_of(place[2] * share, share)
    one = pltpu.make_async_copy(ctf.at[:, pl.ds(first, share)], filters, sems.at[0])
    two = pltpu.make_async_copy(references.at[:, pl.ds(first, share)], part, sems.at[1])
    one.start()
    two.start()
    one.wait()
    two.wait()
    step = 256
    total = jnp.zeros((part.shape[0], EXTRA), jnp.float32)
    for at in range(0, share, step):
        value = part[:, at : at + step]
        table[:, at : at + step] = value
        value = value.astype(jnp.float32)
        value = value * value
        high = rounded(value)
        square = filters[:, at : at + step]
        square = jnp.concatenate(
            list(split3(square * square)) + [jnp.zeros((EXTRA - 3 * group, step), jnp.float32)], axis=0
        ).astype(jnp.bfloat16)
        for some in (high, value - high):
            total = total + lax.dot_general(
                some.astype(jnp.bfloat16), square, (((1,), (1,)), ((), ())), preferred_element_type=jnp.float32
            )
    quad = total + pltpu.roll(total, EXTRA - group, 1) + pltpu.roll(total, EXTRA - 2 * group, 1)
    lane = lax.broadcasted_iota(jnp.int32, quad.shape, 1)
    high, mid, low = split3(jnp.where(lane < group, -0.5 * quad, 0.0))
    table[:, share:] = (high + pltpu.roll(mid, group, 1) + pltpu.roll(low, 2 * group, 1)).astype(jnp.bfloat16)


def share_table(place, references, ctf, shares):
    rows, share = references.shape[0], references.shape[1] // shares
    return pl.pallas_call(
        table_kernel,
        out_shape=jax.ShapeDtypeStruct((rows, share + EXTRA), jnp.bfloat16),
        in_specs=[SMEM, ANY, ANY],
        out_specs=VMEM,
        scratch_shapes=[
            pltpu.VMEM((rows, share), jnp.bfloat16),
            pltpu.VMEM((ctf.shape[0], share), jnp.float32),
            pltpu.SemaphoreType.DMA((2,)),
        ],
        compiler_params=WIDE,
        cost_estimate=pl.CostEstimate(flops=1 << 29, bytes_accessed=8 << 20, transcendentals=0),
    )(place, references, ctf)


def join(blocks, lines):
    at = 0
    for block in blocks:
        lines[at : at + block.shape[0], :] = block[...]
        at += block.shape[0]


def join_kernel(*refs):
    join(refs[:-1], refs[-1])


def score_kernel(counts, *refs):
    count = sum(counts)
    blocks, tables = refs[:count], refs[count : count + 4]
    out, lines = refs[count + 4 :]
    n_dom, rows, width = out.shape[0], out.shape[1], out.shape[2] // 4
    own = rows // len(counts)
    join(blocks, lines)
    share = lines.shape[1] - EXTRA
    extra = lines[:, share:].astype(jnp.float32)
    noise = extra[:, 96:97] + extra[:, 97:98] + extra[:, 98:99]
    for q, table in enumerate(tables):
        part = lax.dot_general(
            lines[...], table[...], (((1,), (1,)), ((), ())), preferred_element_type=jnp.float32
        )
        part = part * noise
        for o in range(len(counts)):
            for d in range(n_dom):
                at = (o * n_dom + d) * own
                out[d, o * own : (o + 1) * own, q * width : (q + 1) * width] = part[at : at + own, :]


def places_of(z_at, rows, own):
    line = lax.broadcasted_iota(jnp.int32, (rows, 2 * rows), 0)
    lane = lax.broadcasted_iota(jnp.int32, (rows, 2 * rows), 1)
    return lane, lax.rem(line + z_at * own, rows)


def soften_kernel(place, parts, score, stats):
    rows = score.shape[0]
    own = rows // stats.shape[0]
    value = parts[0]
    for d in range(1, parts.shape[0]):
        value = value + parts[d]
    score[...] = value
    top = jnp.max(value, axis=1, keepdims=True)
    total = jnp.sum(jnp.exp(value - top), axis=1, keepdims=True)
    lane, target = places_of(place[1], rows, own)
    both = jnp.where(lane == target, top, 0.0) + jnp.where(lane == target + rows, total, 0.0)
    stats[...] = jnp.broadcast_to(jnp.sum(both, axis=0, keepdims=True)[None], stats.shape)


def weigh_kernel(place, score, stats, spread, evidence):
    x_c = place[0]
    rows = score.shape[0]
    tops = stats[...]
    sums = pltpu.roll(tops, rows, 1)
    highest = jnp.max(tops, axis=0, keepdims=True)
    total = jnp.sum(sums * jnp.exp(tops - highest), axis=0, keepdims=True)
    logged = highest + jnp.log(total)
    evidence[...] = logged
    lane, target = places_of(place[1], rows, rows // stats.shape[0])
    column = jnp.sum(jnp.where(lane == target, logged, 0.0), axis=1, keepdims=True)
    value = jnp.exp(score[...] - column).astype(jnp.bfloat16)
    width = value.shape[1] // 4
    for q in range(4):
        part = value[:, q * width : (q + 1) * width]
        for d in range(spread.shape[0] // 4):
            spread[d * 4 + (q ^ x_c)] = part


def renew_kernel(place, spread, square, regularizer, *refs):
    lines, (out, table, weights) = refs[:-3], refs[-3:]
    x_c = place[0]
    n_dom, rows, width = spread.shape[0] // 4, spread.shape[1], spread.shape[2]
    own = 8
    for q in range(4):
        for d in range(n_dom):
            value = spread[d * 4 + (q ^ x_c)].astype(jnp.float32)
            for o in range(rows // own):
                at = (o * n_dom + d) * own
                table[at : at + own, :] = value[o * own : (o + 1) * own, :]
        weights[q * n_dom * rows : (q + 1) * n_dom * rows, :] = table[...].astype(jnp.bfloat16)

    def product(first, span):
        total = jnp.zeros((span, width), jnp.float32)
        at = 0
        for some in lines:
            total = total + lax.dot_general(
                some[:, first : first + span], weights[at : at + some.shape[0], :], (((0,), (0,)), ((), ())), preferred_element_type=jnp.float32
            )
            at += some.shape[0]
        return total

    share = out.shape[0]
    group = square.shape[1] // 4
    high = product(share, EXTRA)[:group]
    first = rounded(high)
    second = (high - first).astype(jnp.bfloat16)
    first = first.astype(jnp.bfloat16)
    factors = jnp.concatenate([first, first, second, jnp.zeros_like(second)], axis=0)
    step = 256
    for at in range(0, share, step):
        bottom = jnp.dot(square[at : at + step, :], factors, preferred_element_type=jnp.float32)
        out[at : at + step, :] = product(at, step) / (bottom + regularizer[...])


def ring_tables(mesh):
    n_ref, n_dom = mesh.shape["ref"], mesh.shape["dom"]
    depth = n_ref // 4

    def along(step):
        return [(i, (i // (2 * depth)) * 2 * depth + (i + 2 * step) % (2 * depth)) for i in range(n_ref)]

    return {
        "core": ("ref", [(i, i ^ 1) for i in range(n_ref)]),
        "side": ("ref", [(i, (i + 2 * depth) % n_ref) for i in range(n_ref)]),
        "up": ("ref", along(1)),
        "down": ("ref", along(-1)),
        "column": [
            [x * 2 * depth + z * 2 + c for z in range(depth)] for x in range(2) for c in range(2)
        ],
        "same_z": [
            [d * n_ref + x * 2 * depth + z * 2 + c for d in range(n_dom) for x in range(2) for c in range(2)]
            for z in range(depth)
        ],
    }


def local(tables, particles, offsets, groups, precision, references, ctf, regularizer):
    def send(name, value):
        axis, pairs = tables[name]
        return lax.ppermute(value, axis, pairs)

    dom = lax.axis_index("dom")
    ref = lax.axis_index("ref")
    n_dom = lax.axis_size("dom")
    n_ref = lax.axis_size("ref")
    depth = n_ref // 4
    x_at, z_at, c_at = ref // (2 * depth), (ref // 2) % depth, ref % 2
    own, pixels = particles.shape
    share = pixels // n_dom
    n_group = ctf.shape[0]
    n_own_ref = references.shape[0]

    pieces = filtered_shares(particles, offsets, groups, precision, ctf, n_dom)

    rows = depth * own
    place = jnp.stack([x_at * 2 + c_at, z_at, dom])
    table = share_table(lax.optimization_barrier((place, pieces))[0], references, ctf, n_dom)
    ctf_share = lax.dynamic_slice_in_dim(ctf, dom * share, share, 1)
    square_t = (ctf_share * ctf_share).T
    square_high = lax.reduce_precision(square_t, 8, 7)
    square = jnp.concatenate(
        [square_high, square_t - square_high, square_high, jnp.zeros_like(square_t)], axis=1
    ).astype(jnp.bfloat16)
    block = lax.all_to_all(pieces, "dom", 0, 0, tiled=True)
    block = block.reshape(n_dom * own, share + EXTRA)
    half = block.shape[0] // 2
    table_x = send("side", lax.optimization_barrier((table, block))[0])
    beside = send("side", block)

    up = [block[:half], block[half:]]
    down = list(up)
    held = {0: [block]}
    for step in range(1, depth // 2):
        for h in range(2):
            sent = (send("up", up[h]), send("down", down[h]))
            up[h], down[h] = lax.optimization_barrier(sent + (up[1 - h], down[1 - h]))[:2]
        held[depth - step] = list(up)
        held[step] = list(down)
    table_x = lax.optimization_barrier((table_x, up[1], down[1]))[0]
    held[depth // 2] = [send("up", up[0]), send("down", down[1])]
    tables4 = [table, send("core", table), table_x, send("core", table_x)]
    blocks = [held[o] for o in range(depth)]
    counts = [len(v) for v in blocks]
    parts, mine = pl.pallas_call(
        functools.partial(score_kernel, counts),
        out_shape=(
            jax.ShapeDtypeStruct((n_dom, rows, 4 * n_own_ref), jnp.float32),
            jax.ShapeDtypeStruct((n_dom * rows, share + EXTRA), jnp.bfloat16),
        ),
        in_specs=[VMEM] * (sum(counts) + 4),
        out_specs=(VMEM, VMEM),
        compiler_params=ROOM,
    )(*[v for some in blocks for v in some], *tables4)
    beside, parts = lax.optimization_barrier((beside, parts))
    parts = lax.all_to_all(parts, "dom", 0, 0, tiled=True)

    up = down = beside
    found = {0: [beside]}
    for step in range(1, depth // 2):
        up, down = send("up", up), send("down", down)
        found[depth - step] = [up]
        found[step] = [down]
    found[depth // 2] = [send("up", up[:half]), send("down", down[half:])]
    found = [v for o in range(depth) for v in found[o]]
    beside = pl.pallas_call(
        join_kernel,
        out_shape=jax.ShapeDtypeStruct((n_dom * rows, share + EXTRA), beside.dtype),
        in_specs=[VMEM] * len(found),
        out_specs=VMEM,
        compiler_params=ROOM,
    )(*found)

    score, stats = pl.pallas_call(
        soften_kernel,
        out_shape=(
            jax.ShapeDtypeStruct((rows, 4 * n_own_ref), jnp.float32),
            jax.ShapeDtypeStruct((depth, 1, 2 * rows), jnp.float32),
        ),
        in_specs=[SMEM, VMEM],
        out_specs=(VMEM, VMEM),
        compiler_params=ROOM,
    )(place, parts)
    stats = lax.all_to_all(stats, "ref", 0, 0, tiled=True, axis_index_groups=tables["column"])
    weights, evidence = pl.pallas_call(
        weigh_kernel,
        out_shape=(
            jax.ShapeDtypeStruct((4 * n_dom, rows, n_own_ref), jnp.bfloat16),
            jax.ShapeDtypeStruct((1, 2 * rows), jnp.float32),
        ),
        in_specs=[SMEM, VMEM, VMEM],
        out_specs=(VMEM, VMEM),
        compiler_params=ROOM,
    )(place, score, stats.reshape(depth, 2 * rows))
    log_evidence = lax.dynamic_slice(evidence, (0, z_at * own), (1, own)).reshape(own)
    weights = lax.all_to_all(
        weights, ("dom", "ref"), 0, 0, tiled=True, axis_index_groups=tables["same_z"]
    )
    lines = [mine, send("core", mine), beside, send("core", beside)]
    new_references = pl.pallas_call(
        renew_kernel,
        out_shape=jax.ShapeDtypeStruct((share, n_own_ref), jnp.float32),
        in_specs=[SMEM] + [VMEM] * (3 + len(lines)),
        out_specs=VMEM,
        scratch_shapes=[
            pltpu.VMEM((n_dom * rows, n_own_ref), jnp.float32),
            pltpu.VMEM((4 * n_dom * rows, n_own_ref), jnp.bfloat16),
        ],
        compiler_params=ROOM,
    )(place, weights, square, regularizer[None, :], *lines)
    return new_references, log_evidence


def solution(mesh):
    return jax.shard_map(
        functools.partial(local, ring_tables(mesh)),
        mesh=mesh,
        in_specs=(
            P(("dom", "ref"), None),
            P(("dom", "ref"), None),
            P(("dom", "ref")),
            P(("dom", "ref")),
            P("ref", None),
            P(),
            P("ref"),
        ),
        out_specs=(P("dom", "ref"), P(("dom", "ref"))),
        check_vma=False,
    )
```

```python
import functools

import jax
import jax.numpy as jnp
import numpy as np
from jax import lax
from jax.experimental import pallas as pl
from jax.experimental.pallas import tpu as pltpu
from jax.sharding import PartitionSpec as P

IMG = 128
EXTRA = 128


VMEM = pl.BlockSpec(memory_space=pltpu.VMEM)
SMEM = pl.BlockSpec(memory_space=pltpu.SMEM)
ANY = pl.BlockSpec(memory_space=pl.ANY)
LESS = pltpu.CompilerParams(vmem_limit_bytes=16 << 20)
ROOM = pltpu.CompilerParams(vmem_limit_bytes=24 << 20)
WIDE = pltpu.CompilerParams(vmem_limit_bytes=56 << 20)


def rounded(value):
    return value.astype(jnp.bfloat16).astype(jnp.float32)


def split3(value):
    high = rounded(value)
    rest = value - high
    mid = rounded(rest)
    return high, mid, rest - mid


def filter_kernel(offsets, groups, precision, particles, ctf, out, planes, images, rows, sems):
    count, side = images.shape[0], IMG
    shares, _, width = out.shape
    pixels = width - EXTRA
    per_share = pixels // side
    whole = pltpu.make_async_copy(particles, images, sems.at[count])
    whole.start()
    copies = []
    for n in range(count):
        copy = pltpu.make_async_copy(ctf.at[pl.ds(groups[n], 1)], rows.at[pl.ds(n, 1)], sems.at[n])
        copy.start()
        copies.append(copy)
    lane = lax.broadcasted_iota(jnp.int32, (1, EXTRA), 1)
    slot = lax.broadcasted_iota(jnp.int32, (count, EXTRA), 0)
    extra = jnp.zeros((count, EXTRA), jnp.float32)
    for n in range(count):
        hot = jnp.where((lane < 96) & (lax.rem(lane, 32) == groups[n]), 1.0, 0.0)
        for part, value in enumerate(split3(jnp.full((1, EXTRA), precision[n], jnp.float32))):
            hot = jnp.where(lane == 96 + part, value, hot)
        extra = jnp.where(slot == n, hot, extra)
    extra = extra.astype(jnp.bfloat16)
    whole.wait()
    for line in range(side):
        planes[pl.ds(line, count, stride=side), :] = images[
            :, line * side : (line + 1) * side
        ].astype(jnp.float32)
    for n in range(count):
        image = planes[n * side : (n + 1) * side, :]
        image = pltpu.roll(image, lax.rem(offsets[0, n] + side, side), 0)
        image = pltpu.roll(image, lax.rem(offsets[1, n] + side, side), 1)
        planes[n * side : (n + 1) * side, :] = image
    for copy in copies:
        copy.wait()
    for share in range(shares):
        for line in range(per_share):
            at = share * per_share + line
            value = planes[pl.ds(at, count, stride=side), :] * rows[:, at * side : (at + 1) * side]
            out[share, :, line * side : (line + 1) * side] = value.astype(jnp.bfloat16)
        out[share, :, pixels:] = extra


def filtered_shares(particles, offsets, groups, precision, ctf, shares):
    images, pixels = particles.shape
    return pl.pallas_call(
        filter_kernel,
        out_shape=jax.ShapeDtypeStruct((shares, images, pixels // shares + EXTRA), jnp.bfloat16),
        in_specs=[SMEM, SMEM, SMEM, ANY, ANY],
        out_specs=VMEM,
        scratch_shapes=[
            pltpu.VMEM((images * IMG, IMG), jnp.float32),
            pltpu.VMEM((images, pixels), jnp.bfloat16),
            pltpu.VMEM((images, pixels), jnp.float32),
            pltpu.SemaphoreType.DMA((images + 1,)),
        ],
        compiler_params=WIDE,
    )(offsets.T, groups, precision, particles, ctf)


def table_kernel(place, references, ctf, table, part, filters, sems):
    share = part.shape[1]
    group = ctf.shape[0]
    first = pl.multiple_of(place[2] * share, share)
    one = pltpu.make_async_copy(ctf.at[:, pl.ds(first, share)], filters, sems.at[0])
    two = pltpu.make_async_copy(references.at[:, pl.ds(first, share)], part, sems.at[1])
    one.start()
    two.start()
    one.wait()
    two.wait()
    step = 256
    total = jnp.zeros((part.shape[0], EXTRA), jnp.float32)
    for at in range(0, share, step):
        value = part[:, at : at + step]
        table[:, at : at + step] = value
        value = value.astype(jnp.float32)
        value = value * value
        high = rounded(value)
        square = filters[:, at : at + step]
        square = jnp.concatenate(
            list(split3(square * square)) + [jnp.zeros((EXTRA - 3 * group, step), jnp.float32)], axis=0
        ).astype(jnp.bfloat16)
        for some in (high, value - high):
            total = total + lax.dot_general(
                some.astype(jnp.bfloat16), square, (((1,), (1,)), ((), ())), preferred_element_type=jnp.float32
            )
    quad = total + pltpu.roll(total, EXTRA - group, 1) + pltpu.roll(total, EXTRA - 2 * group, 1)
    lane = lax.broadcasted_iota(jnp.int32, quad.shape, 1)
    high, mid, low = split3(jnp.where(lane < group, -0.5 * quad, 0.0))
    table[:, share:] = (high + pltpu.roll(mid, group, 1) + pltpu.roll(low, 2 * group, 1)).astype(jnp.bfloat16)


def share_table(place, references, ctf, shares):
    rows, share = references.shape[0], references.shape[1] // shares
    return pl.pallas_call(
        table_kernel,
        out_shape=jax.ShapeDtypeStruct((rows, share + EXTRA), jnp.bfloat16),
        in_specs=[SMEM, ANY, ANY],
        out_specs=VMEM,
        scratch_shapes=[
            pltpu.VMEM((rows, share), jnp.bfloat16),
            pltpu.VMEM((ctf.shape[0], share), jnp.float32),
            pltpu.SemaphoreType.DMA((2,)),
        ],
        compiler_params=WIDE,
        cost_estimate=pl.CostEstimate(flops=1 << 29, bytes_accessed=8 << 20, transcendentals=0),
    )(place, references, ctf)


def join(blocks, lines):
    at = 0
    for block in blocks:
        lines[at : at + block.shape[0], :] = block[...]
        at += block.shape[0]


def join_kernel(*refs):
    join(refs[:-1], refs[-1])


def score_kernel(counts, *refs):
    count = sum(counts)
    blocks, tables = refs[:count], refs[count : count + 4]
    out, lines = refs[count + 4 :]
    n_dom, rows, width = out.shape[0], out.shape[1], out.shape[2] // 4
    own = rows // len(counts)
    join(blocks, lines)
    share = lines.shape[1] - EXTRA
    extra = lines[:, share:].astype(jnp.float32)
    noise = extra[:, 96:97] + extra[:, 97:98] + extra[:, 98:99]
    for q, table in enumerate(tables):
        part = lax.dot_general(
            lines[...], table[...], (((1,), (1,)), ((), ())), preferred_element_type=jnp.float32
        )
        part = part * noise
        for o in range(len(counts)):
            for d in range(n_dom):
                at = (o * n_dom + d) * own
                out[d, o * own : (o + 1) * own, q * width : (q + 1) * width] = part[at : at + own, :]


def places_of(z_at, rows, own):
    line = lax.broadcasted_iota(jnp.int32, (rows, 2 * rows), 0)
    lane = lax.broadcasted_iota(jnp.int32, (rows, 2 * rows), 1)
    return lane, lax.rem(line + z_at * own, rows)


def soften_kernel(place, parts, score, stats):
    rows = score.shape[0]
    own = rows // stats.shape[0]
    value = parts[0]
    for d in range(1, parts.shape[0]):
        value = value + parts[d]
    score[...] = value
    top = jnp.max(value, axis=1, keepdims=True)
    total = jnp.sum(jnp.exp(value - top), axis=1, keepdims=True)
    lane, target = places_of(place[1], rows, own)
    both = jnp.where(lane == target, top, 0.0) + jnp.where(lane == target + rows, total, 0.0)
    stats[...] = jnp.broadcast_to(jnp.sum(both, axis=0, keepdims=True)[None], stats.shape)


def weigh_kernel(place, score, stats, spread, evidence):
    x_c = place[0]
    rows = score.shape[0]
    tops = stats[...]
    sums = pltpu.roll(tops, rows, 1)
    highest = jnp.max(tops, axis=0, keepdims=True)
    total = jnp.sum(sums * jnp.exp(tops - highest), axis=0, keepdims=True)
    logged = highest + jnp.log(total)
    evidence[...] = logged
    lane, target = places_of(place[1], rows, rows // stats.shape[0])
    column = jnp.sum(jnp.where(lane == target, logged, 0.0), axis=1, keepdims=True)
    value = jnp.exp(score[...] - column).astype(jnp.bfloat16)
    width = value.shape[1] // 4
    for q in range(4):
        part = value[:, q * width : (q + 1) * width]
        for d in range(spread.shape[0] // 4):
            spread[d * 4 + (q ^ x_c)] = part


def renew_kernel(place, spread, square, regularizer, *refs):
    lines, (out, table, weights) = refs[:-3], refs[-3:]
    x_c = place[0]
    n_dom, rows, width = spread.shape[0] // 4, spread.shape[1], spread.shape[2]
    own = 8
    for q in range(4):
        for d in range(n_dom):
            value = spread[d * 4 + (q ^ x_c)].astype(jnp.float32)
            for o in range(rows // own):
                at = (o * n_dom + d) * own
                table[at : at + own, :] = value[o * own : (o + 1) * own, :]
        weights[q * n_dom * rows : (q + 1) * n_dom * rows, :] = table[...].astype(jnp.bfloat16)

    def product(first, span):
        total = jnp.zeros((span, width), jnp.float32)
        at = 0
        for some in lines:
            total = total + lax.dot_general(
                some[:, first : first + span], weights[at : at + some.shape[0], :], (((0,), (0,)), ((), ())), preferred_element_type=jnp.float32
            )
            at += some.shape[0]
        return total

    share = out.shape[0]
    group = square.shape[1] // 4
    high = product(share, EXTRA)[:group]
    first = rounded(high)
    second = (high - first).astype(jnp.bfloat16)
    first = first.astype(jnp.bfloat16)
    factors = jnp.concatenate([first, first, second, jnp.zeros_like(second)], axis=0)
    step = 256
    for at in range(0, share, step):
        bottom = jnp.dot(square[at : at + step, :], factors, preferred_element_type=jnp.float32)
        out[at : at + step, :] = product(at, step) / (bottom + regularizer[...])


def ring_tables(mesh):
    n_ref, n_dom = mesh.shape["ref"], mesh.shape["dom"]
    depth = n_ref // 4

    def along(step):
        return [(i, (i // (2 * depth)) * 2 * depth + (i + 2 * step) % (2 * depth)) for i in range(n_ref)]

    return {
        "core": ("ref", [(i, i ^ 1) for i in range(n_ref)]),
        "side": ("ref", [(i, (i + 2 * depth) % n_ref) for i in range(n_ref)]),
        "up": ("ref", along(1)),
        "down": ("ref", along(-1)),
        "column": [
            [x * 2 * depth + z * 2 + c for z in range(depth)] for x in range(2) for c in range(2)
        ],
        "same_z": [
            [d * n_ref + x * 2 * depth + z * 2 + c for d in range(n_dom) for x in range(2) for c in range(2)]
            for z in range(depth)
        ],
    }


def local(tables, particles, offsets, groups, precision, references, ctf, regularizer):
    def send(name, value):
        axis, pairs = tables[name]
        return lax.ppermute(value, axis, pairs)

    dom = lax.axis_index("dom")
    ref = lax.axis_index("ref")
    n_dom = lax.axis_size("dom")
    n_ref = lax.axis_size("ref")
    depth = n_ref // 4
    x_at, z_at, c_at = ref // (2 * depth), (ref // 2) % depth, ref % 2
    own, pixels = particles.shape
    share = pixels // n_dom
    n_group = ctf.shape[0]
    n_own_ref = references.shape[0]

    pieces = filtered_shares(particles, offsets, groups, precision, ctf, n_dom)

    rows = depth * own
    place = jnp.stack([x_at * 2 + c_at, z_at, dom])
    table = share_table(lax.optimization_barrier((place, pieces))[0], references, ctf, n_dom)
    ctf_share = lax.dynamic_slice_in_dim(ctf, dom * share, share, 1)
    square_t = (ctf_share * ctf_share).T
    square_high = lax.reduce_precision(square_t, 8, 7)
    square = jnp.concatenate(
        [square_high, square_t - square_high, square_high, jnp.zeros_like(square_t)], axis=1
    ).astype(jnp.bfloat16)
    block = lax.all_to_all(pieces, "dom", 0, 0, tiled=True)
    block = block.reshape(n_dom * own, share + EXTRA)
    half = block.shape[0] // 2
    table_x = send("side", lax.optimization_barrier((table, block))[0])
    beside = send("side", block)

    up = down = block
    held = {0: [block]}
    for step in range(1, depth // 2):
        up, down = send("up", up), send("down", down)
        held[depth - step] = [up]
        held[step] = [down]
    table_x = lax.optimization_barrier((table_x, up, down))[0]
    held[depth // 2] = [send("up", up[:half]), send("down", down[half:])]
    tables4 = [table, send("core", table), table_x, send("core", table_x)]
    blocks = [held[o] for o in range(depth)]
    counts = [len(v) for v in blocks]
    parts, mine = pl.pallas_call(
        functools.partial(score_kernel, counts),
        out_shape=(
            jax.ShapeDtypeStruct((n_dom, rows, 4 * n_own_ref), jnp.float32),
            jax.ShapeDtypeStruct((n_dom * rows, share + EXTRA), jnp.bfloat16),
        ),
        in_specs=[VMEM] * (sum(counts) + 4),
        out_specs=(VMEM, VMEM),
        compiler_params=ROOM,
    )(*[v for some in blocks for v in some], *tables4)
    beside, parts = lax.optimization_barrier((beside, parts))
    parts = lax.all_to_all(parts, "dom", 0, 0, tiled=True)

    up = down = beside
    found = {0: [beside]}
    for step in range(1, depth // 2):
        up, down = send("up", up), send("down", down)
        found[depth - step] = [up]
        found[step] = [down]
    found[depth // 2] = [send("up", up[:half]), send("down", down[half:])]
    found = [v for o in range(depth) for v in found[o]]
    beside = pl.pallas_call(
        join_kernel,
        out_shape=jax.ShapeDtypeStruct((n_dom * rows, share + EXTRA), beside.dtype),
        in_specs=[VMEM] * len(found),
        out_specs=VMEM,
        compiler_params=ROOM,
    )(*found)

    score, stats = pl.pallas_call(
        soften_kernel,
        out_shape=(
            jax.ShapeDtypeStruct((rows, 4 * n_own_ref), jnp.float32),
            jax.ShapeDtypeStruct((depth, 1, 2 * rows), jnp.float32),
        ),
        in_specs=[SMEM, VMEM],
        out_specs=(VMEM, VMEM),
        compiler_params=LESS,
    )(place, parts)
    stats = lax.all_to_all(stats, "ref", 0, 0, tiled=True, axis_index_groups=tables["column"])
    weights, evidence = pl.pallas_call(
        weigh_kernel,
        out_shape=(
            jax.ShapeDtypeStruct((4 * n_dom, rows, n_own_ref), jnp.bfloat16),
            jax.ShapeDtypeStruct((1, 2 * rows), jnp.float32),
        ),
        in_specs=[SMEM, VMEM, VMEM],
        out_specs=(VMEM, VMEM),
        compiler_params=ROOM,
    )(place, score, stats.reshape(depth, 2 * rows))
    log_evidence = lax.dynamic_slice(evidence, (0, z_at * own), (1, own)).reshape(own)
    weights = lax.all_to_all(
        weights, ("dom", "ref"), 0, 0, tiled=True, axis_index_groups=tables["same_z"]
    )
    lines = [mine, send("core", mine), beside, send("core", beside)]
    new_references = pl.pallas_call(
        renew_kernel,
        out_shape=jax.ShapeDtypeStruct((share, n_own_ref), jnp.float32),
        in_specs=[SMEM] + [VMEM] * (3 + len(lines)),
        out_specs=VMEM,
        scratch_shapes=[
            pltpu.VMEM((n_dom * rows, n_own_ref), jnp.float32),
            pltpu.VMEM((4 * n_dom * rows, n_own_ref), jnp.bfloat16),
        ],
        compiler_params=ROOM,
    )(place, weights, square, regularizer[None, :], *lines)
    return new_references, log_evidence


def solution(mesh):
    return jax.shard_map(
        functools.partial(local, ring_tables(mesh)),
        mesh=mesh,
        in_specs=(
            P(("dom", "ref"), None),
            P(("dom", "ref"), None),
            P(("dom", "ref")),
            P(("dom", "ref")),
            P("ref", None),
            P(),
            P("ref"),
        ),
        out_specs=(P("dom", "ref"), P(("dom", "ref"))),
        check_vma=False,
    )
```

```python
import functools

import jax
import jax.numpy as jnp
import numpy as np
from jax import lax
from jax.experimental import pallas as pl
from jax.experimental.pallas import tpu as pltpu
from jax.sharding import PartitionSpec as P

IMG = 128
EXTRA = 128


VMEM = pl.BlockSpec(memory_space=pltpu.VMEM)
SMEM = pl.BlockSpec(memory_space=pltpu.SMEM)
ANY = pl.BlockSpec(memory_space=pl.ANY)
LESS = pltpu.CompilerParams(vmem_limit_bytes=16 << 20)
ROOM = pltpu.CompilerParams(vmem_limit_bytes=24 << 20)
WIDE = pltpu.CompilerParams(vmem_limit_bytes=56 << 20)


def rounded(value):
    return value.astype(jnp.bfloat16).astype(jnp.float32)


def split3(value):
    high = rounded(value)
    rest = value - high
    mid = rounded(rest)
    return high, mid, rest - mid


def filter_kernel(offsets, groups, precision, particles, ctf, out, planes, images, rows, sems):
    count, side = images.shape[0], IMG
    shares, _, width = out.shape
    pixels = width - EXTRA
    per_share = pixels // side
    whole = pltpu.make_async_copy(particles, images, sems.at[count])
    whole.start()
    copies = []
    for n in range(count):
        copy = pltpu.make_async_copy(ctf.at[pl.ds(groups[n], 1)], rows.at[pl.ds(n, 1)], sems.at[n])
        copy.start()
        copies.append(copy)
    lane = lax.broadcasted_iota(jnp.int32, (1, EXTRA), 1)
    slot = lax.broadcasted_iota(jnp.int32, (count, EXTRA), 0)
    extra = jnp.zeros((count, EXTRA), jnp.float32)
    for n in range(count):
        hot = jnp.where((lane < 96) & (lax.rem(lane, 32) == groups[n]), 1.0, 0.0)
        for part, value in enumerate(split3(jnp.full((1, EXTRA), precision[n], jnp.float32))):
            hot = jnp.where(lane == 96 + part, value, hot)
        extra = jnp.where(slot == n, hot, extra)
    extra = extra.astype(jnp.bfloat16)
    whole.wait()
    for line in range(side):
        planes[pl.ds(line, count, stride=side), :] = images[
            :, line * side : (line + 1) * side
        ].astype(jnp.float32)
    for n in range(count):
        image = planes[n * side : (n + 1) * side, :]
        image = pltpu.roll(image, lax.rem(offsets[0, n] + side, side), 0)
        image = pltpu.roll(image, lax.rem(offsets[1, n] + side, side), 1)
        planes[n * side : (n + 1) * side, :] = image
    for copy in copies:
        copy.wait()
    for share in range(shares):
        for line in range(per_share):
            at = share * per_share + line
            value = planes[pl.ds(at, count, stride=side), :] * rows[:, at * side : (at + 1) * side]
            out[share, :, line * side : (line + 1) * side] = value.astype(jnp.bfloat16)
        out[share, :, pixels:] = extra


def filtered_shares(particles, offsets, groups, precision, ctf, shares):
    images, pixels = particles.shape
    return pl.pallas_call(
        filter_kernel,
        out_shape=jax.ShapeDtypeStruct((shares, images, pixels // shares + EXTRA), jnp.bfloat16),
        in_specs=[SMEM, SMEM, SMEM, ANY, ANY],
        out_specs=VMEM,
        scratch_shapes=[
            pltpu.VMEM((images * IMG, IMG), jnp.float32),
            pltpu.VMEM((images, pixels), jnp.bfloat16),
            pltpu.VMEM((images, pixels), jnp.float32),
            pltpu.SemaphoreType.DMA((images + 1,)),
        ],
        compiler_params=WIDE,
    )(offsets.T, groups, precision, particles, ctf)


def table_kernel(place, references, ctf, table, part, filters, sems):
    share = part.shape[1]
    group = ctf.shape[0]
    first = pl.multiple_of(place[2] * share, share)
    one = pltpu.make_async_copy(ctf.at[:, pl.ds(first, share)], filters, sems.at[0])
    two = pltpu.make_async_copy(references.at[:, pl.ds(first, share)], part, sems.at[1])
    one.start()
    two.start()
    one.wait()
    two.wait()
    step = 256
    total = jnp.zeros((part.shape[0], EXTRA), jnp.float32)
    for at in range(0, share, step):
        value = part[:, at : at + step]
        table[:, at : at + step] = value
        value = value.astype(jnp.float32)
        value = value * value
        high = rounded(value)
        square = filters[:, at : at + step]
        square = jnp.concatenate(
            list(split3(square * square)) + [jnp.zeros((EXTRA - 3 * group, step), jnp.float32)], axis=0
        ).astype(jnp.bfloat16)
        for some in (high, value - high):
            total = total + lax.dot_general(
                some.astype(jnp.bfloat16), square, (((1,), (1,)), ((), ())), preferred_element_type=jnp.float32
            )
    quad = total + pltpu.roll(total, EXTRA - group, 1) + pltpu.roll(total, EXTRA - 2 * group, 1)
    lane = lax.broadcasted_iota(jnp.int32, quad.shape, 1)
    high, mid, low = split3(jnp.where(lane < group, -0.5 * quad, 0.0))
    table[:, share:] = (high + pltpu.roll(mid, group, 1) + pltpu.roll(low, 2 * group, 1)).astype(jnp.bfloat16)


def share_table(place, references, ctf, shares):
    rows, share = references.shape[0], references.shape[1] // shares
    return pl.pallas_call(
        table_kernel,
        out_shape=jax.ShapeDtypeStruct((rows, share + EXTRA), jnp.bfloat16),
        in_specs=[SMEM, ANY, ANY],
        out_specs=VMEM,
        scratch_shapes=[
            pltpu.VMEM((rows, share), jnp.bfloat16),
            pltpu.VMEM((ctf.shape[0], share), jnp.float32),
            pltpu.SemaphoreType.DMA((2,)),
        ],
        compiler_params=WIDE,
        cost_estimate=pl.CostEstimate(flops=1 << 29, bytes_accessed=8 << 20, transcendentals=0),
    )(place, references, ctf)


def join(blocks, lines):
    at = 0
    for block in blocks:
        lines[at : at + block.shape[0], :] = block[...]
        at += block.shape[0]


def join_kernel(*refs):
    join(refs[:-1], refs[-1])


def score_kernel(counts, *refs):
    count = sum(counts)
    blocks, tables = refs[:count], refs[count : count + 4]
    out, lines = refs[count + 4 :]
    n_dom, rows, width = out.shape[0], out.shape[1], out.shape[2] // 4
    own = rows // len(counts)
    join(blocks, lines)
    share = lines.shape[1] - EXTRA
    extra = lines[:, share:].astype(jnp.float32)
    noise = extra[:, 96:97] + extra[:, 97:98] + extra[:, 98:99]
    for q, table in enumerate(tables):
        part = lax.dot_general(
            lines[...], table[...], (((1,), (1,)), ((), ())), preferred_element_type=jnp.float32
        )
        part = part * noise
        for o in range(len(counts)):
            for d in range(n_dom):
                at = (o * n_dom + d) * own
                out[d, o * own : (o + 1) * own, q * width : (q + 1) * width] = part[at : at + own, :]


def places_of(z_at, rows, own):
    line = lax.broadcasted_iota(jnp.int32, (rows, 2 * rows), 0)
    lane = lax.broadcasted_iota(jnp.int32, (rows, 2 * rows), 1)
    return lane, lax.rem(line + z_at * own, rows)


def soften_kernel(place, parts, score, stats):
    rows = score.shape[0]
    own = rows // stats.shape[0]
    value = parts[0]
    for d in range(1, parts.shape[0]):
        value = value + parts[d]
    score[...] = value
    top = jnp.max(value, axis=1, keepdims=True)
    total = jnp.sum(jnp.exp(value - top), axis=1, keepdims=True)
    lane, target = places_of(place[1], rows, own)
    both = jnp.where(lane == target, top, 0.0) + jnp.where(lane == target + rows, total, 0.0)
    stats[...] = jnp.broadcast_to(jnp.sum(both, axis=0, keepdims=True)[None], stats.shape)


def weigh_kernel(place, score, stats, spread, evidence):
    x_c = place[0]
    rows = score.shape[0]
    tops = stats[...]
    sums = pltpu.roll(tops, rows, 1)
    highest = jnp.max(tops, axis=0, keepdims=True)
    total = jnp.sum(sums * jnp.exp(tops - highest), axis=0, keepdims=True)
    logged = highest + jnp.log(total)
    evidence[...] = logged
    lane, target = places_of(place[1], rows, rows // stats.shape[0])
    column = jnp.sum(jnp.where(lane == target, logged, 0.0), axis=1, keepdims=True)
    value = jnp.exp(score[...] - column).astype(jnp.bfloat16)
    width = value.shape[1] // 4
    for q in range(4):
        part = value[:, q * width : (q + 1) * width]
        for d in range(spread.shape[0] // 4):
            spread[d * 4 + (q ^ x_c)] = part


def renew_kernel(orders, place, spread, square, regularizer, *refs):
    lines, (out, table, weights) = refs[:-3], refs[-3:]
    x_c = place[0]
    n_dom, rows, width = spread.shape[0] // 4, spread.shape[1], spread.shape[2]
    own = rows // len(orders[0])
    for q in range(4):
        for d in range(n_dom):
            value = spread[d * 4 + (q ^ x_c)].astype(jnp.float32)
            for k, o in enumerate(orders[q]):
                at = (k * n_dom + d) * own
                table[at : at + own, :] = value[o * own : (o + 1) * own, :]
        weights[q * n_dom * rows : (q + 1) * n_dom * rows, :] = table[...].astype(jnp.bfloat16)

    def product(first, span):
        total, at = 0.0, 0
        for some in lines:
            total = total + lax.dot_general(
                some[:, first : first + span],
                weights[at : at + some.shape[0], :],
                (((0,), (0,)), ((), ())),
                preferred_element_type=jnp.float32,
            )
            at += some.shape[0]
        return total

    share = out.shape[0]
    group = square.shape[1] // 4
    high = product(share, EXTRA)[:group]
    first = rounded(high)
    second = (high - first).astype(jnp.bfloat16)
    first = first.astype(jnp.bfloat16)
    factors = jnp.concatenate([first, first, second, jnp.zeros_like(second)], axis=0)
    step = 256
    for at in range(0, share, step):
        bottom = jnp.dot(square[at : at + step, :], factors, preferred_element_type=jnp.float32)
        out[at : at + step, :] = product(at, step) / (bottom + regularizer[...])


def ring_tables(mesh):
    n_ref, n_dom = mesh.shape["ref"], mesh.shape["dom"]
    depth = n_ref // 4

    def along(step):
        return [(i, (i // (2 * depth)) * 2 * depth + (i + 2 * step) % (2 * depth)) for i in range(n_ref)]

    return {
        "core": ("ref", [(i, i ^ 1) for i in range(n_ref)]),
        "side": ("ref", [(i, (i + 2 * depth) % n_ref) for i in range(n_ref)]),
        "up": ("ref", along(1)),
        "down": ("ref", along(-1)),
        "column": [
            [x * 2 * depth + z * 2 + c for z in range(depth)] for x in range(2) for c in range(2)
        ],
        "same_z": [
            [d * n_ref + x * 2 * depth + z * 2 + c for d in range(n_dom) for x in range(2) for c in range(2)]
            for z in range(depth)
        ],
    }


def local(tables, particles, offsets, groups, precision, references, ctf, regularizer):
    def send(name, value):
        axis, pairs = tables[name]
        return lax.ppermute(value, axis, pairs)

    dom = lax.axis_index("dom")
    ref = lax.axis_index("ref")
    n_dom = lax.axis_size("dom")
    n_ref = lax.axis_size("ref")
    depth = n_ref // 4
    x_at, z_at, c_at = ref // (2 * depth), (ref // 2) % depth, ref % 2
    own, pixels = particles.shape
    share = pixels // n_dom
    n_group = ctf.shape[0]
    n_own_ref = references.shape[0]

    pieces = filtered_shares(particles, offsets, groups, precision, ctf, n_dom)

    rows = depth * own
    place = jnp.stack([x_at * 2 + c_at, z_at, dom])
    table = share_table(lax.optimization_barrier((place, pieces))[0], references, ctf, n_dom)
    ctf_share = lax.dynamic_slice_in_dim(ctf, dom * share, share, 1)
    square_t = (ctf_share * ctf_share).T
    square_high = lax.reduce_precision(square_t, 8, 7)
    square = jnp.concatenate(
        [square_high, square_t - square_high, square_high, jnp.zeros_like(square_t)], axis=1
    ).astype(jnp.bfloat16)
    block = lax.all_to_all(pieces, "dom", 0, 0, tiled=True)
    block = block.reshape(n_dom * own, share + EXTRA)
    half = block.shape[0] // 2
    table_x = send("side", lax.optimization_barrier((table, block))[0])
    beside = send("side", block)

    up = down = block
    held = {0: [block]}
    for step in range(1, depth // 2):
        up, down = send("up", up), send("down", down)
        held[depth - step] = [up]
        held[step] = [down]
    table_x = lax.optimization_barrier((table_x, up, down))[0]
    held[depth // 2] = [send("up", up[:half]), send("down", down[half:])]
    tables4 = [table, send("core", table), table_x, send("core", table_x)]
    blocks = [held[o] for o in range(depth)]
    counts = [len(v) for v in blocks]
    parts, mine = pl.pallas_call(
        functools.partial(score_kernel, counts),
        out_shape=(
            jax.ShapeDtypeStruct((n_dom, rows, 4 * n_own_ref), jnp.float32),
            jax.ShapeDtypeStruct((n_dom * rows, share + EXTRA), jnp.bfloat16),
        ),
        in_specs=[VMEM] * (sum(counts) + 4),
        out_specs=(VMEM, VMEM),
        compiler_params=ROOM,
    )(*[v for some in blocks for v in some], *tables4)
    beside, parts = lax.optimization_barrier((beside, parts))
    parts = lax.all_to_all(parts, "dom", 0, 0, tiled=True)

    reach = depth // 4
    up = down = beside
    found = {0: beside}
    for step in range(1, reach + 1):
        up, down = send("up", up), send("down", down)
        found[depth - step] = up
        found[step] = down
    near = sorted(found)
    far = [o for o in range(depth) if o not in found]
    lowest, own_rows = far[0] * n_dom * own, len(far) * n_dom * own
    found = [found[o] for o in near]
    beside = pl.pallas_call(
        join_kernel,
        out_shape=jax.ShapeDtypeStruct((sum(v.shape[0] for v in found), share + EXTRA), mine.dtype),
        in_specs=[VMEM] * len(found),
        out_specs=VMEM,
        compiler_params=ROOM,
    )(*found)

    parts, beside = lax.optimization_barrier((parts, beside))
    score, stats = pl.pallas_call(
        soften_kernel,
        out_shape=(
            jax.ShapeDtypeStruct((rows, 4 * n_own_ref), jnp.float32),
            jax.ShapeDtypeStruct((depth, 1, 2 * rows), jnp.float32),
        ),
        in_specs=[SMEM, VMEM],
        out_specs=(VMEM, VMEM),
        compiler_params=LESS,
    )(place, parts)
    distant = lax.slice_in_dim(mine, lowest, lowest + own_rows)
    distant, score = lax.optimization_barrier((distant, score))
    distant = send("side", distant)
    stats = lax.all_to_all(stats, "ref", 0, 0, tiled=True, axis_index_groups=tables["column"])
    weights, evidence = pl.pallas_call(
        weigh_kernel,
        out_shape=(
            jax.ShapeDtypeStruct((4 * n_dom, rows, n_own_ref), jnp.bfloat16),
            jax.ShapeDtypeStruct((1, 2 * rows), jnp.float32),
        ),
        in_specs=[SMEM, VMEM, VMEM],
        out_specs=(VMEM, VMEM),
        compiler_params=ROOM,
    )(place, score, stats.reshape(depth, 2 * rows))
    log_evidence = lax.dynamic_slice(evidence, (0, z_at * own), (1, own)).reshape(own)
    weights = lax.all_to_all(
        weights, ("dom", "ref"), 0, 0, tiled=True, axis_index_groups=tables["same_z"]
    )
    lines = [mine, send("core", mine), beside, distant, send("core", beside), send("core", distant)]
    natural, order = list(range(depth)), near + far
    new_references = pl.pallas_call(
        functools.partial(renew_kernel, (natural, natural, order, order)),
        out_shape=jax.ShapeDtypeStruct((share, n_own_ref), jnp.float32),
        in_specs=[SMEM] + [VMEM] * (3 + len(lines)),
        out_specs=VMEM,
        scratch_shapes=[
            pltpu.VMEM((n_dom * rows, n_own_ref), jnp.float32),
            pltpu.VMEM((4 * n_dom * rows, n_own_ref), jnp.bfloat16),
        ],
        compiler_params=ROOM,
    )(place, weights, square, regularizer[None, :], *lines)
    return new_references, log_evidence


def solution(mesh):
    return jax.shard_map(
        functools.partial(local, ring_tables(mesh)),
        mesh=mesh,
        in_specs=(
            P(("dom", "ref"), None),
            P(("dom", "ref"), None),
            P(("dom", "ref")),
            P(("dom", "ref")),
            P("ref", None),
            P(),
            P("ref"),
        ),
        out_specs=(P("dom", "ref"), P(("dom", "ref"))),
        check_vma=False,
    )
```
